32 devices in a mesh: groups: 2 (over x), mem: 16 (over z, y, core).
Axes of the slice: x: 2, y: 2, z: 4, core: 2. Of those that a mesh axis runs over, the one named last changes fastest.
Arguments:
- hidden: bfloat16 [16384, 2560], P(('groups', 'mem')), parts along dimension 0, may hold values from -6 to 6
- cotangent: bfloat16 [16384, 2560], P(('groups', 'mem')), parts along dimension 0, may hold values from -6 to 6
- hash_ids: int32 [16384, 4], P(('groups', 'mem')), parts along dimension 0, may hold values from 0 to 16383, as said below
- seq_lengths: int32 [32, 4], P(('groups', 'mem')), parts along dimension 0, may hold values from 1 to 256, 512 in all within a row
- hash_table: bfloat16 [16384, 128], P('mem'), may hold values from -6 to 6
- w_key: bfloat16 [512, 2560], replicated, may hold values from -0.25 to 0.25
- w_value: bfloat16 [512, 2560], replicated, may hold values from -0.25 to 0.25
- conv_weight: float32 [4, 2560], replicated, may hold values from -3 to 3
Outputs:
- new_hidden: bfloat16 [16384, 2560], P(('groups', 'mem')), parts along dimension 0
- grad_hidden: bfloat16 [16384, 2560], P(('groups', 'mem')), parts along dimension 0
- table_grad: float32 [32768, 128], P(('groups', 'mem')), parts along dimension 0
The draws below stay inside these ranges and needn't reach their ends.
There are 2 independent parts, one for each index of `groups`. The reference program is written for one: setup_inputs(seed, part) draws one part's arguments, and reference() takes and returns one part's arrays. A program takes and returns all parts, laid end to end along the dimension named above; an argument that names none is the same for every part. Nothing has to cross between parts.
Inputs may be any that keep to these rules, and one draw needn't show every extreme that they name: `hash_ids`: row r lies in table block r // 1024. Among the 2048 ids of one device's tokens at most 256 lie in any one block; one block receives exactly 256 from every device's tokens.
All inputs are finite; a program needn't handle non-finite values.
Results may differ from the reference program's by a relative error of at most 0.0028.
Values may be sent and summed in bfloat16 or wider, within the bound.
A program may use at most 128 MiB of HBM per device.

```python
import math
import jax
import jax.numpy as jnp
import numpy as np
from jax import lax

D = 2560
HEADS = 4
ROW = 128
KW = 4
SEQS = 4
TOK_DEV = 512
R_DEV = 1024
SHARDS = 16
TOKENS = 8192
TABLE_ROWS = 16384
CAP = 256


def draw_hash_ids(key, part):
    key = jax.random.fold_in(key, 11)
    first_key, second_key, third_key = jax.random.split(key, 3)
    per_block = TOK_DEV * HEADS
    hottest = jax.random.randint(first_key, (), 0, SHARDS)
    counter = jnp.arange(per_block, dtype=jnp.int32)
    spread = (hottest + 1 + (counter - CAP) % (SHARDS - 1)) % SHARDS
    pattern = jnp.where(counter < CAP, hottest, spread).astype(jnp.int32)
    block_keys = jax.random.split(second_key, SHARDS)
    owners = jax.vmap(lambda block_key: jax.random.permutation(block_key, pattern))(block_keys)
    offsets = jax.random.randint(third_key, (SHARDS, per_block), 0, R_DEV)
    return (owners * R_DEV + offsets).reshape(TOKENS, HEADS).astype(jnp.int32)


def steps_of(key, extent, cuts, low, top_value):
    loudness = 1.0
    for dim, shards_of in cuts:
        draws = jax.random.uniform(jax.random.fold_in(jax.random.fold_in(key, 6), dim), (shards_of,), jnp.float32, low / len(cuts), top_value / len(cuts))
        loudness = loudness * jnp.repeat(jnp.exp(draws), extent[dim] // shards_of).reshape((-1,) + (1,) * (len(extent) - 1 - dim))
    return loudness


def split_up(count, total, most, slope):
    weights = [(1 << 20) // math.isqrt(rank ** slope) + 1 for rank in range(2, count + 1)]
    spare, given = total - most - (count - 1), [1] * (count - 1)
    while spare > 0:
        free = [i for i in range(count - 1) if given[i] < most]
        pool, left = sum([weights[i] for i in free]), spare
        for i in free:
            more = min(most - given[i], max(1, left * weights[i] // pool), spare)
            given[i] = given[i] + more
            spare = spare - more
    return np.array([most] + given)


def uneven_parts(key, number_of, total, limit, skew):
    if number_of == 2:
        one = jax.random.randint(key, (), max(1, total - limit), min(limit, total - 1) + 1)
        return jnp.stack([one, total - one])
    sizes = jnp.asarray(split_up(number_of, total, limit, skew), jnp.int32)
    twos = (number_of - 1) // 2
    source_of, receiver = sizes[1:1 + 2 * twos:2], sizes[2:2 + 2 * twos:2]
    slack = jnp.minimum(source_of - 1, limit - receiver)
    moved = jax.random.randint(jax.random.fold_in(key, 1), (twos,), 0, 1 << 20) % (slack + 1)
    sizes = sizes.at[1:1 + 2 * twos:2].set(source_of - moved).at[2:2 + 2 * twos:2].set(receiver + moved)
    return sizes[jax.random.permutation(jax.random.fold_in(key, 2), number_of)]


def bell_draw(own_key, dims, scale, limit, pieces=(), kind=jnp.bfloat16):
    entries = scale * jax.random.normal(own_key, dims, jnp.float32)
    if pieces:
        entries = entries * steps_of(own_key, dims, pieces, -0.22, 0.18)
    return jnp.clip(entries, -limit, limit).astype(kind)


def setup_inputs(seed: int = 0, part: int = 0) -> dict:
    key_of = jax.random.split(jax.random.key(seed), 9)
    part_splits = jax.random.split(jax.random.fold_in(key_of[8], part), 9)
    return {
        "hidden": bell_draw(part_splits[0], (TOKENS, D), 1.0, 6.0, ((0, 16),)),
        "cotangent": bell_draw(part_splits[1], (TOKENS, D), 1.0, 6.0, ((0, 16),)),
        "hash_ids": draw_hash_ids(jax.random.fold_in(jax.random.fold_in(key_of[8], part), 71), part),
        "seq_lengths": jax.vmap(lambda own: uneven_parts(own, SEQS, TOK_DEV, TOK_DEV // 2, 0))(jax.random.split(part_splits[3], SHARDS)).reshape((SHARDS, SEQS)).astype(jnp.int32),
        "hash_table": bell_draw(key_of[4], (TABLE_ROWS, ROW), 1.0, 6.0, ((0, 16),)),
        "w_key": bell_draw(key_of[5], (HEADS * ROW, D), (HEADS * ROW) ** -0.5, 0.25),
        "w_value": bell_draw(key_of[6], (HEADS * ROW, D), (HEADS * ROW) ** -0.5, 0.25),
        "conv_weight": bell_draw(key_of[7], (KW, D), 0.5, 3.0, (), jnp.float32),
    }


epsilon = 1e-06

def rms_scaled(vectors):
    return vectors * lax.rsqrt(lax.optimization_barrier(jnp.mean(vectors * vectors, axis=-1, keepdims=True)) + epsilon)

def positions(seq_lengths, block_len):
    seq_ends = jnp.cumsum(seq_lengths, axis=1).astype(jnp.int32)
    steps_in = jnp.arange(block_len, dtype=jnp.int32)
    before = (seq_ends[:, None, :] <= steps_in[None, :, None]).astype(jnp.int32)
    starts = lax.optimization_barrier(jnp.sum(before * seq_lengths[:, None, :], axis=2)).astype(jnp.int32)
    return (steps_in[None, :] - starts).reshape(-1).astype(jnp.int32)

def layer_part(hidden32, key_proj, value_proj, conv_weight, within):
    columns = hidden32.shape[1]
    scores = lax.optimization_barrier(jnp.sum(rms_scaled(hidden32) * rms_scaled(key_proj), axis=1, keepdims=True)) / math.sqrt(columns)
    carried = jax.nn.sigmoid(scores) * value_proj
    convolved = jnp.zeros_like(carried)
    for offset in range(conv_weight.shape[0]):
        delayed = jnp.pad(carried, ((offset, 0), (0, 0)))[:carried.shape[0]]
        convolved = convolved + conv_weight[offset] * jnp.where((within >= offset)[:, None], delayed, 0.0)
    return hidden32 + carried + jax.nn.silu(convolved)

def back_project(grads, weight):
    return lax.dot_general(grads, weight, (((1,), (1,)), ((), ())), preferred_element_type=jnp.float32)

def reference(hidden, cotangent, hash_ids, seq_lengths, hash_table, w_key, w_value, conv_weight):
    fetched = jnp.take(hash_table, hash_ids.reshape(-1), axis=0).reshape(TOKENS, HEADS * ROW)
    key_proj = jnp.dot(fetched, w_key, preferred_element_type=jnp.float32)
    value_proj = jnp.dot(fetched, w_value, preferred_element_type=jnp.float32)
    within = positions(seq_lengths, TOK_DEV)

    def forward(hidden32, keys_in, values_in):
        return layer_part(hidden32, keys_in, values_in, conv_weight, within)
    output, pullback = jax.vjp(forward, hidden.astype(jnp.float32), key_proj, value_proj)
    d_hidden, d_key, d_value = pullback(cotangent.astype(jnp.float32))
    d_fetched = back_project(d_key.astype(jnp.bfloat16), w_key) + back_project(d_value.astype(jnp.bfloat16), w_value)
    table_grad = jnp.zeros((TABLE_ROWS, ROW), jnp.float32).at[hash_ids.reshape(-1)].add(d_fetched.reshape(-1, ROW))
    return (output.astype(jnp.bfloat16), d_hidden.astype(jnp.bfloat16), table_grad)
```

```python
import functools
import math

import jax
import jax.numpy as jnp
from jax import lax
from jax.experimental import pallas as pl
from jax.experimental.pallas import tpu as pltpu
from jax.sharding import PartitionSpec as P

epsilon = 1e-06
LANES = 128
bf16 = jnp.bfloat16
f32 = jnp.float32
i32 = jnp.int32
NT = (((1,), (1,)), ((), ()))


def dot(a, b, dims=(((1,), (0,)), ((), ()))):
    return lax.dot_general(a, b, dims, preferred_element_type=f32)


def iota(shape, dim):
    return lax.broadcasted_iota(i32, shape, dim)


def one_hot(match):
    return jnp.where(match, 1.0, 0.0).astype(bf16)


def partner(me, step, shards):
    total, bit = 0, 1
    while bit < shards:
        total = total + (((me // bit) % 2 + (step // bit) % 2) % 2) * bit
        bit *= 2
    return total


def greet(me, shards):
    barrier = pltpu.get_barrier_semaphore()

    def tell(step, carry):
        pl.semaphore_signal(barrier, inc=1, device_id={"mem": partner(me, step, shards)})
        return carry

    lax.fori_loop(1, shards, tell, 0)
    pl.semaphore_wait(barrier, shards - 1)


def as_column(row):
    return jnp.transpose(jnp.broadcast_to(row, (LANES, row.shape[1])))


def fetch_kernel(shards, cap, ids_ref, table_ref, fetched_ref, slots_ref, asked_ref,
                 requests, answers, replies, columns, total,
                 ask_send, ask_recv, row_send, row_recv):
    me = lax.axis_index("mem")
    heads, tokens = ids_ref.shape
    rows = table_ref.shape[0]
    wide = requests.shape[2]

    def ask(peer):
        return pltpu.make_async_remote_copy(
            src_ref=requests.at[peer], dst_ref=asked_ref.at[me],
            send_sem=ask_send.at[peer], recv_sem=ask_recv.at[me], device_id={"mem": peer})

    def asked_by(peer):
        return pltpu.make_async_remote_copy(
            src_ref=requests.at[peer], dst_ref=asked_ref.at[peer],
            send_sem=ask_send.at[peer], recv_sem=ask_recv.at[peer], device_id={"mem": peer})

    def reply(peer):
        return pltpu.make_async_remote_copy(
            src_ref=answers.at[peer], dst_ref=replies.at[me],
            send_sem=row_send.at[peer], recv_sem=row_recv.at[me], device_id={"mem": peer})

    def reply_of(peer):
        return pltpu.make_async_remote_copy(
            src_ref=answers.at[peer], dst_ref=replies.at[peer],
            send_sem=row_send.at[peer], recv_sem=row_recv.at[peer], device_id={"mem": peer})

    earlier = one_hot(iota((tokens, tokens), 0) < iota((tokens, tokens), 1))
    seen = jnp.zeros((shards, 1), f32)
    gathered = jnp.zeros((3 * shards, wide), f32)
    for h in range(heads):
        ids = ids_ref[h:h + 1, :]
        owner = ids // rows
        offset = ids - owner * rows
        mine = jnp.where(jnp.broadcast_to(owner, (shards, tokens)) == iota((shards, tokens), 0), 1.0, 0.0)
        ranks = dot(mine.astype(bf16), earlier) + seen
        seen = seen + jnp.sum(mine, axis=1, keepdims=True)
        rank = jnp.sum(mine * ranks, axis=0, keepdims=True).astype(i32)
        slot = owner * cap + rank
        slots_ref[h:h + 1, :] = slot
        columns[h] = as_column(slot)
        at_rank = one_hot(jnp.broadcast_to(rank, (wide, tokens)) == iota((wide, tokens), 0))
        high = (offset // 256).astype(f32)
        low = (offset % 256).astype(f32)
        parts = jnp.concatenate([mine * high, mine * low, mine], axis=0).astype(bf16)
        gathered = gathered + dot(parts, at_rank, NT)
    wanted = gathered[:shards] * 256.0 + gathered[shards:2 * shards]
    wanted = jnp.where(gathered[2 * shards:] > 0.5, wanted, -1.0).astype(i32)
    for peer in range(shards):
        requests[peer] = wanted[peer:peer + 1, :]

    greet(me, shards)

    def ask_all(j, carry):
        ask(partner(me, shards - j, shards)).start()
        return carry

    lax.fori_loop(1, shards, ask_all, 0)
    asked_ref[me] = requests[me]

    def rows_for(peer):
        column = as_column(asked_ref[peer])[:cap]
        hot = jnp.concatenate(
            [one_hot(column == iota((cap, LANES), 1) + start) for start in range(0, rows, LANES)], axis=1)
        return dot(hot, table_ref[...]).astype(bf16)

    def answer(j, carry):
        peer = partner(me, shards - j, shards)
        asked_by(peer).wait_recv()
        answers[peer] = rows_for(peer)
        reply(peer).start()
        return carry

    lax.fori_loop(1, shards, answer, 0)
    replies[me] = rows_for(me)

    def unpack(peer):
        block = replies[peer]
        for h in range(heads):
            base = peer * cap
            column = columns[h] - base
            if cap % LANES == 0:
                hot = jnp.concatenate(
                    [one_hot(column == iota((tokens, LANES), 1) + start) for start in range(0, cap, LANES)], axis=1)
            else:
                hot = one_hot(column == iota((tokens, LANES), 1))[:, :cap]
            total[:, h * LANES:(h + 1) * LANES] += dot(hot, block)

    total[...] = jnp.zeros_like(total)
    unpack(me)

    def take(step, carry):
        peer = partner(me, step, shards)
        reply_of(peer).wait_recv()
        unpack(peer)
        return carry

    lax.fori_loop(1, shards, take, 0)
    fetched_ref[...] = total[...].astype(bf16)

    def finish(step, carry):
        peer = partner(me, step, shards)
        ask(peer).wait_send()
        reply(peer).wait_send()
        return carry

    lax.fori_loop(1, shards, finish, 0)


def fetch(ids, table, shards, cap):
    heads, tokens = ids.shape
    width = table.shape[1]
    wide = max(cap, LANES)
    vmem = pl.BlockSpec(memory_space=pltpu.VMEM)
    return pl.pallas_call(
        functools.partial(fetch_kernel, shards, cap),
        out_shape=(
            jax.ShapeDtypeStruct((tokens, heads * width), bf16),
            jax.ShapeDtypeStruct((heads, tokens), i32),
            jax.ShapeDtypeStruct((shards, 1, wide), i32),
        ),
        in_specs=[vmem, vmem],
        out_specs=(vmem, vmem, vmem),
        scratch_shapes=[
            pltpu.VMEM((shards, 1, wide), i32),
            pltpu.VMEM((shards, cap, width), bf16),
            pltpu.VMEM((shards, cap, width), bf16),
            pltpu.VMEM((heads, tokens, LANES), i32),
            pltpu.VMEM((tokens, heads * width), f32),
            pltpu.SemaphoreType.DMA((shards,)),
            pltpu.SemaphoreType.DMA((shards,)),
            pltpu.SemaphoreType.DMA((shards,)),
            pltpu.SemaphoreType.DMA((shards,)),
        ],
        compiler_params=pltpu.CompilerParams(
            collective_id=0, has_side_effects=True, vmem_limit_bytes=24 * 2**20),
        name="fetch",
    )(ids, table)


def layer_kernel(lengths_ref, fetched_ref, hidden_ref, cotangent_ref, wk_ref, wv_ref, conv_ref,
                 out_ref, grad_ref, pieces_ref,
                 keys, values, dvalues, dkeys, masks, ahead, carried, dconv,
                 sums, gates, dgate, total):
    tokens, columns = hidden_ref.shape
    taps = conv_ref.shape[0]
    shape = (tokens, LANES)
    block = 512 if columns % 512 == 0 else LANES
    chunk = 128

    def within(position):
        start = jnp.zeros(shape, i32)
        end = 0
        for s in range(lengths_ref.shape[1]):
            length = lengths_ref[0, s]
            end = end + length
            start = start + jnp.where(position >= end, length, 0)
        return position - start

    here = iota(shape, 0)
    for k in range(1, taps):
        masks[k - 1] = jnp.where(within(here) >= k, 1.0, 0.0)
        ahead[k - 1] = jnp.where((within(here + k) >= k) & (here + k < tokens), 1.0, 0.0)
    sums[...] = jnp.zeros_like(sums)
    dgate[...] = jnp.zeros_like(dgate)
    carried[0:8] = jnp.zeros((8, LANES), f32)
    dconv[tokens:tokens + 8] = jnp.zeros((8, LANES), f32)

    def project(j, carry):
        at = pl.ds(pl.multiple_of(j * block, block), block)
        key = dot(fetched_ref[...], wk_ref[:, at])
        keys[:, at] = key
        values[:, at] = dot(fetched_ref[...], wv_ref[:, at])
        for c in range(0, block, LANES):
            hid = hidden_ref[:, pl.ds(pl.multiple_of(j * block + c, LANES), LANES)].astype(f32)
            part = key[:, c:c + LANES]
            sums[0] += part * part
            sums[1] += part * hid
            sums[2] += hid * hid
        return carry

    lax.fori_loop(0, columns // block, project, 0)
    inv = 1.0 / columns
    k_scale = lax.rsqrt(jnp.sum(sums[0], axis=1, keepdims=True) * inv + epsilon)
    h_scale = lax.rsqrt(jnp.sum(sums[2], axis=1, keepdims=True) * inv + epsilon)
    cross = jnp.sum(sums[1], axis=1, keepdims=True)
    score = cross * k_scale * h_scale * (1.0 / math.sqrt(columns))
    gate = 0.5 + 0.5 * jnp.tanh(0.5 * score)
    gates[...] = jnp.broadcast_to(gate, shape)

    def mix(j, carry):
        at = pl.ds(pl.multiple_of(j * LANES, LANES), LANES)
        w = [conv_ref[k:k + 1, at] for k in range(taps)]
        for r in range(0, tokens, chunk):
            carried[8 + r:8 + r + chunk] = gates[r:r + chunk] * values[r:r + chunk, at]
        for r in range(0, tokens, chunk):
            now = carried[8 + r:8 + r + chunk]
            conv = w[0] * now
            for k in range(1, taps):
                conv = conv + w[k] * (masks[k - 1, r:r + chunk] * carried[8 + r - k:8 + r - k + chunk])
            sig = 0.5 + 0.5 * jnp.tanh(0.5 * conv)
            silu = conv * sig
            out_ref[r:r + chunk, at] = (hidden_ref[r:r + chunk, at].astype(f32) + now + silu).astype(bf16)
            dconv[r:r + chunk] = cotangent_ref[r:r + chunk, at].astype(f32) * (sig + silu * (1.0 - sig))
        for r in range(0, tokens, chunk):
            dcarried = cotangent_ref[r:r + chunk, at].astype(f32) + w[0] * dconv[r:r + chunk]
            for k in range(1, taps):
                dcarried = dcarried + w[k] * (ahead[k - 1, r:r + chunk] * dconv[r + k:r + k + chunk])
            dvalues[r:r + chunk, at] = (gates[r:r + chunk] * dcarried).astype(bf16)
            dgate[r:r + chunk] += values[r:r + chunk, at] * dcarried
        return carry

    lax.fori_loop(0, columns // LANES, mix, 0)
    dscore = jnp.sum(dgate[...], axis=1, keepdims=True) * gate * (1.0 - gate) * (1.0 / math.sqrt(columns))
    both = dscore * k_scale * h_scale
    sums[0] = jnp.broadcast_to(both, shape)
    sums[1] = jnp.broadcast_to(both * h_scale * h_scale * cross * inv, shape)
    sums[2] = jnp.broadcast_to(both * k_scale * k_scale * cross * inv, shape)
    total[...] = jnp.zeros_like(total)

    def back(j, carry):
        at = pl.ds(pl.multiple_of(j * block, block), block)
        for c in range(0, block, LANES):
            col = pl.ds(pl.multiple_of(j * block + c, LANES), LANES)
            for r in range(0, tokens, chunk):
                row = slice(r, r + chunk)
                hid = hidden_ref[row, col].astype(f32)
                key = keys[row, col]
                a = sums[0, row]
                grad_ref[row, col] = (
                    cotangent_ref[row, col].astype(f32) + (a * key - sums[1, row] * hid)).astype(bf16)
                dkeys[row, c:c + LANES] = (a * hid - sums[2, row] * key).astype(bf16)
        total[...] += dot(dkeys[...], wk_ref[:, at], NT) + dot(dvalues[:, at], wv_ref[:, at], NT)
        return carry

    lax.fori_loop(0, columns // block, back, 0)
    pieces_ref[...] = total[...].astype(bf16)


def layer(lengths, fetched, hidden, cotangent, w_key, w_value, conv_weight):
    tokens, columns = hidden.shape
    depth = fetched.shape[1]
    taps = conv_weight.shape[0]
    vmem = pl.BlockSpec(memory_space=pltpu.VMEM)
    block = 512 if columns % 512 == 0 else LANES
    return pl.pallas_call(
        layer_kernel,
        out_shape=(
            jax.ShapeDtypeStruct((tokens, columns), bf16),
            jax.ShapeDtypeStruct((tokens, columns), bf16),
            jax.ShapeDtypeStruct((tokens, depth), bf16),
        ),
        in_specs=[pl.BlockSpec(memory_space=pltpu.SMEM)] + [vmem] * 6,
        out_specs=(vmem, vmem, vmem),
        scratch_shapes=[
            pltpu.VMEM((tokens, columns), f32),
            pltpu.VMEM((tokens, columns), f32),
            pltpu.VMEM((tokens, columns), bf16),
            pltpu.VMEM((tokens, block), bf16),
            pltpu.VMEM((taps - 1, tokens, LANES), f32),
            pltpu.VMEM((taps - 1, tokens, LANES), f32),
            pltpu.VMEM((tokens + 8, LANES), f32),
            pltpu.VMEM((tokens + 8, LANES), f32),
            pltpu.VMEM((3, tokens, LANES), f32),
            pltpu.VMEM((tokens, LANES), f32),
            pltpu.VMEM((tokens, LANES), f32),
            pltpu.VMEM((tokens, depth), f32),
        ],
        compiler_params=pltpu.CompilerParams(vmem_limit_bytes=48 * 2**20),
        name="layer",
    )(lengths, fetched, hidden, cotangent, w_key, w_value, conv_weight)


def spread_kernel(shards, cap, slots_ref, asked_ref, pieces_ref, grad_ref, outgoing, incoming, send, recv):
    me = lax.axis_index("mem")
    heads, tokens = slots_ref.shape
    rows = grad_ref.shape[0]

    def push(peer):
        return pltpu.make_async_remote_copy(
            src_ref=outgoing.at[peer], dst_ref=incoming.at[me],
            send_sem=send.at[peer], recv_sem=recv.at[me], device_id={"mem": peer})

    def pushed_by(peer):
        return pltpu.make_async_remote_copy(
            src_ref=outgoing.at[peer], dst_ref=incoming.at[peer],
            send_sem=send.at[peer], recv_sem=recv.at[peer], device_id={"mem": peer})

    def pack(peer):
        packed = jnp.zeros((cap, LANES), f32)
        for h in range(heads):
            row = slots_ref[h:h + 1, :] - peer * cap
            hot = one_hot(jnp.broadcast_to(row, (cap, tokens)) == iota((cap, tokens), 0))
            packed = packed + dot(hot, pieces_ref[:, h * LANES:(h + 1) * LANES])
        return packed.astype(bf16)

    greet(me, shards)

    def send_one(j, carry):
        peer = partner(me, shards - j, shards)
        outgoing[peer] = pack(peer)
        push(peer).start()
        return carry

    lax.fori_loop(1, shards, send_one, 0)
    incoming[me] = pack(me)

    def add(peer):
        row = asked_ref[peer][:, :cap]
        hot = one_hot(jnp.broadcast_to(row, (rows, cap)) == iota((rows, cap), 0))
        return dot(hot, incoming[peer])

    grad_ref[...] = add(me)

    def take(step, carry):
        peer = partner(me, step, shards)
        pushed_by(peer).wait_recv()
        grad_ref[...] += add(peer)
        return carry

    lax.fori_loop(1, shards, take, 0)

    def finish(step, carry):
        push(partner(me, step, shards)).wait_send()
        return carry

    lax.fori_loop(1, shards, finish, 0)


def spread(slots, asked, pieces, rows, shards, cap):
    vmem = pl.BlockSpec(memory_space=pltpu.VMEM)
    return pl.pallas_call(
        functools.partial(spread_kernel, shards, cap),
        out_shape=jax.ShapeDtypeStruct((rows, LANES), f32),
        in_specs=[vmem] * 3,
        out_specs=vmem,
        scratch_shapes=[
            pltpu.VMEM((shards, cap, LANES), bf16),
            pltpu.VMEM((shards, cap, LANES), bf16),
            pltpu.SemaphoreType.DMA((shards,)),
            pltpu.SemaphoreType.DMA((shards,)),
        ],
        compiler_params=pltpu.CompilerParams(
            collective_id=1, has_side_effects=True, vmem_limit_bytes=24 * 2**20),
        name="spread",
    )(slots, asked, pieces)


def local(hidden, cotangent, hash_ids, seq_lengths, hash_table, w_key, w_value, conv_weight):
    shards = lax.axis_size("mem")
    cap = 2 * hash_ids.size // shards
    fetched, slots, asked = fetch(hash_ids.T, hash_table, shards, cap)
    new_hidden, grad_hidden, pieces = layer(
        seq_lengths, fetched, hidden, cotangent, w_key, w_value, conv_weight)
    table_grad = spread(slots, asked, pieces, hash_table.shape[0], shards, cap)
    return new_hidden, grad_hidden, table_grad


def solution(mesh):
    tokens = P(("groups", "mem"), None)
    return jax.shard_map(
        local,
        mesh=mesh,
        in_specs=(tokens, tokens, tokens, tokens, P("mem", None), P(), P(), P()),
        out_specs=(tokens, tokens, tokens),
        check_vma=False,
    )
```

```python
import functools
import math

import jax
import jax.numpy as jnp
from jax import lax
from jax.experimental import pallas as pl
from jax.experimental.pallas import tpu as pltpu
from jax.sharding import PartitionSpec as P

epsilon = 1e-06
LANES = 128
LAYER_VMEM = 60 * 2**20
SWAP_VMEM = 60 * 2**20
bf16 = jnp.bfloat16
f32 = jnp.float32
i32 = jnp.int32
NT = (((1,), (1,)), ((), ()))


def dot(a, b, dims=(((1,), (0,)), ((), ()))):
    return lax.dot_general(a, b, dims, preferred_element_type=f32)


def iota(shape, dim):
    return lax.broadcasted_iota(i32, shape, dim)


def one_hot(match):
    return jnp.where(match, 1.0, 0.0).astype(bf16)


def partner(me, step, shards):
    total, bit = 0, 1
    while bit < shards:
        total = total + (((me // bit) % 2 + (step // bit) % 2) % 2) * bit
        bit *= 2
    return total


def greet(peers):
    barrier = pltpu.get_barrier_semaphore()
    for peer in peers:
        pl.semaphore_signal(barrier, inc=1, device_id=peer)
    pl.semaphore_wait(barrier, len(peers))


def as_column(row):
    return jnp.transpose(jnp.broadcast_to(row, (LANES, row.shape[1])))


def fetch_kernel(shards, cap, ids_hbm, table_hbm, fetched_ref, slots_ref, asked_ref,
                 table, mirror, requests, asks, answers, replies, columns, total,
                 ask_send, ask_recv, row_send, row_recv, far_send, far_recv, swap_send, swap_recv,
                 tell_send, tell_recv, table_sem, ids_ref, ids_sem):
    me, group = lax.axis_index("mem"), lax.axis_index("groups")
    groups = lax.axis_size("groups")
    half = shards // 2
    home = me // half
    opposite = partner(me, half, shards)
    heads, tokens = ids_ref.shape
    rows = table.shape[0]
    wide = requests.shape[3]
    far = {"mem": opposite}
    twin = {"groups": partner(group, 1, 2) + (group // 2) * 2}
    share = rows // 2 if groups % 2 == 0 else rows
    mine_at = pl.ds(pl.multiple_of((group % 2) * share, 16), share) if share < rows else pl.ds(0, rows)
    twin_at = pl.ds(pl.multiple_of((1 - group % 2) * share, 16), share)

    def remote(src, dst, send, recv, device):
        return pltpu.make_async_remote_copy(
            src_ref=src, dst_ref=dst, send_sem=send, recv_sem=recv, device_id=device)

    def ask(peer, slot):
        at = peer % half
        return remote(requests.at[:, at], asks.at[:, slot], ask_send.at[at], ask_recv.at[slot], {"mem": peer})

    def reply(peer, side, slot):
        at = peer % half
        return remote(answers.at[side, at], replies.at[side, slot],
                      row_send.at[side, at], row_recv.at[side, slot], {"mem": peer})

    here = me % half
    ids_load = pltpu.make_async_copy(ids_hbm, ids_ref, ids_sem)
    ids_load.start()
    greet([{"mem": partner(me, step, shards)} for step in range(1, half)] + [far]
          + ([twin] if share < rows else []))
    to_far = remote(table_hbm.at[mine_at], mirror.at[mine_at], far_send, far_recv, far)
    to_far.start()
    table_load = pltpu.make_async_copy(table_hbm, table, table_sem)
    table_load.start()
    ids_load.wait()

    earlier = one_hot(iota((tokens, tokens), 0) < iota((tokens, tokens), 1))
    seen = jnp.zeros((shards, 1), f32)
    gathered = jnp.zeros((3 * shards, wide), f32)
    for h in range(heads):
        ids = ids_ref[h:h + 1, :]
        owner = ids // rows
        offset = ids - owner * rows
        mine = jnp.where(jnp.broadcast_to(owner, (shards, tokens)) == iota((shards, tokens), 0), 1.0, 0.0)
        ranks = dot(mine.astype(bf16), earlier) + seen
        seen = seen + jnp.sum(mine, axis=1, keepdims=True)
        rank = jnp.sum(mine * ranks, axis=0, keepdims=True).astype(i32)
        slot = owner * cap + rank
        slots_ref[h:h + 1, :] = slot
        columns[h] = as_column(slot)
        at_rank = one_hot(jnp.broadcast_to(rank, (wide, tokens)) == iota((wide, tokens), 0))
        high = (offset // 256).astype(f32)
        low = (offset % 256).astype(f32)
        parts = jnp.concatenate([mine * high, mine * low, mine], axis=0).astype(bf16)
        gathered = gathered + dot(parts, at_rank, NT)
    wanted = gathered[:shards] * 256.0 + gathered[shards:2 * shards]
    wanted = jnp.where(gathered[2 * shards:] > 0.5, wanted, -1.0).astype(i32)
    for block in range(shards):
        requests[(block // half + home) % 2, block % half] = wanted[block:block + 1, :]

    def ask_all(j, carry):
        ask(partner(me, half - j, shards), here).start()
        return carry

    lax.fori_loop(1, half, ask_all, 0)
    asks[:, here] = requests[:, here]
    table_load.wait()

    def rows_for(side, peer, held):
        column = as_column(asks[side, peer % half])[:cap]
        hot = jnp.concatenate(
            [one_hot(column == iota((cap, LANES), 1) + start) for start in range(0, rows, LANES)], axis=1)
        return dot(hot, held[...]).astype(bf16)

    def answer(j, carry):
        peer = partner(me, half - j, shards)
        ask(peer, peer % half).wait_recv()
        answers[0, peer % half] = rows_for(0, peer, table)
        reply(peer, 0, here).start()
        return carry

    lax.fori_loop(1, half, answer, 0)
    asked_ref[0] = asks[0]
    tell = remote(asks.at[1], asked_ref.at[1], tell_send, tell_recv, far)
    tell.start()

    to_far.wait_recv()
    if share < rows:
        swap = remote(mirror.at[mine_at], mirror.at[mine_at], swap_send, swap_recv, twin)
        swap.start()
    replies[0, here] = rows_for(0, me, table)

    def unpack(side, peer):
        block = replies[side, peer % half]
        base = ((home + side) % 2 * half + peer % half) * cap
        for h in range(heads):
            column = columns[h] - base
            if cap % LANES == 0:
                hot = jnp.concatenate(
                    [one_hot(column == iota((tokens, LANES), 1) + start) for start in range(0, cap, LANES)], axis=1)
            else:
                hot = one_hot(column == iota((tokens, LANES), 1))[:, :cap]
            total[:, h * LANES:(h + 1) * LANES] += dot(hot, block)

    total[...] = jnp.zeros_like(total)
    unpack(0, me)
    if share < rows:
        remote(mirror.at[twin_at], mirror.at[twin_at], swap_send, swap_recv, twin).wait_recv()

    def answer_far(j, carry):
        peer = partner(me, half - j, shards)
        answers[1, peer % half] = rows_for(1, peer, mirror)
        reply(peer, 1, here).start()
        return carry

    lax.fori_loop(1, half, answer_far, 0)
    replies[1, here] = rows_for(1, me, mirror)
    unpack(1, me)

    for side in range(2):
        def take(step, carry):
            peer = partner(me, step, shards)
            reply(peer, side, peer % half).wait_recv()
            unpack(side, peer)
            return carry

        lax.fori_loop(1, half, take, 0)
    fetched_ref[...] = total[...].astype(bf16)

    def finish(step, carry):
        peer = partner(me, step, shards)
        ask(peer, here).wait_send()
        reply(peer, 0, here).wait_send()
        reply(peer, 1, here).wait_send()
        return carry

    lax.fori_loop(1, half, finish, 0)
    to_far.wait_send()
    if share < rows:
        swap.wait_send()
    tell.wait()


def fetch(ids, table, shards, cap):
    heads, tokens = ids.shape
    rows, width = table.shape
    wide = max(cap, LANES)
    half = shards // 2
    vmem = pl.BlockSpec(memory_space=pltpu.VMEM)
    anywhere = pl.BlockSpec(memory_space=pltpu.HBM)
    dma = pltpu.SemaphoreType.DMA
    return pl.pallas_call(
        functools.partial(fetch_kernel, shards, cap),
        out_shape=(
            jax.ShapeDtypeStruct((tokens, heads * width), bf16),
            jax.ShapeDtypeStruct((heads, tokens), i32),
            jax.ShapeDtypeStruct((2, half, 1, wide), i32),
        ),
        in_specs=[anywhere] * 2,
        out_specs=(vmem, vmem, vmem),
        scratch_shapes=[
            pltpu.VMEM((rows, width), bf16),
            pltpu.VMEM((rows, width), bf16),
            pltpu.VMEM((2, half, 1, wide), i32),
            pltpu.VMEM((2, half, 1, wide), i32),
            pltpu.VMEM((2, half, cap, width), bf16),
            pltpu.VMEM((2, half, cap, width), bf16),
            pltpu.VMEM((heads, tokens, LANES), i32),
            pltpu.VMEM((tokens, heads * width), f32),
            dma((half,)), dma((half,)), dma((2, half)), dma((2, half)),
            dma, dma, dma, dma, dma, dma,
            dma, pltpu.VMEM((heads, tokens), i32), dma,
        ],
        compiler_params=pltpu.CompilerParams(
            collective_id=0, has_side_effects=True, vmem_limit_bytes=SWAP_VMEM),
        name="fetch",
    )(ids, table)


def layer_kernel(lengths_ref, fetched_ref, hidden_hbm, cotangent_hbm, wk_hbm, wv_hbm, conv_hbm,
                 out_hbm, grad_hbm, pieces_ref,
                 hidden_ref, cotangent_ref, wk_ref, wv_ref, conv_ref, load_sem, conv_sem,
                 out_ref, grad_ref, out_sem, grad_sem, keys, values, dvalues, dkeys, masks, ahead, carried, dconv,
                 sums, gates, dgate, total):
    tokens, columns = hidden_ref.shape
    taps = conv_ref.shape[0]
    shape = (tokens, LANES)
    block = 512 if columns % 512 == 0 else LANES
    chunk = 128

    def load(which, j):
        src, dst = ((wk_hbm, wk_ref), (wv_hbm, wv_ref), (hidden_hbm, hidden_ref),
                    (cotangent_hbm, cotangent_ref))[which]
        at = pl.ds(pl.multiple_of(j * block, block), block)
        return pltpu.make_async_copy(src.at[:, at], dst.at[:, at], load_sem.at[which, j])

    for j in range(columns // block):
        for which in range(3):
            load(which, j).start()
    conv_load = pltpu.make_async_copy(conv_hbm, conv_ref, conv_sem)
    conv_load.start()
    for j in range(columns // block):
        load(3, j).start()

    def within(position):
        start = jnp.zeros(shape, i32)
        end = 0
        for s in range(lengths_ref.shape[1]):
            length = lengths_ref[0, s]
            end = end + length
            start = start + jnp.where(position >= end, length, 0)
        return position - start

    here = iota(shape, 0)
    for k in range(1, taps):
        masks[k - 1] = jnp.where(within(here) >= k, 1.0, 0.0)
        ahead[k - 1] = jnp.where((within(here + k) >= k) & (here + k < tokens), 1.0, 0.0)
    sums[...] = jnp.zeros_like(sums)
    dgate[...] = jnp.zeros_like(dgate)
    carried[0:8] = jnp.zeros((8, LANES), f32)
    dconv[tokens:tokens + 8] = jnp.zeros((8, LANES), f32)

    def project(j, carry):
        at = pl.ds(pl.multiple_of(j * block, block), block)
        for which in range(3):
            load(which, j).wait()
        key = dot(fetched_ref[...], wk_ref[:, at])
        keys[:, at] = key
        values[:, at] = dot(fetched_ref[...], wv_ref[:, at])
        for c in range(0, block, LANES):
            hid = hidden_ref[:, pl.ds(pl.multiple_of(j * block + c, LANES), LANES)].astype(f32)
            part = key[:, c:c + LANES]
            sums[0] += part * part
            sums[1] += part * hid
            sums[2] += hid * hid
        return carry

    lax.fori_loop(0, columns // block, project, 0)
    inv = 1.0 / columns
    k_scale = lax.rsqrt(jnp.sum(sums[0], axis=1, keepdims=True) * inv + epsilon)
    h_scale = lax.rsqrt(jnp.sum(sums[2], axis=1, keepdims=True) * inv + epsilon)
    cross = jnp.sum(sums[1], axis=1, keepdims=True)
    score = cross * k_scale * h_scale * (1.0 / math.sqrt(columns))
    gate = 0.5 + 0.5 * jnp.tanh(0.5 * score)
    gates[...] = jnp.broadcast_to(gate, shape)

    def write(src, dst, sems, j):
        at = pl.ds(pl.multiple_of(j * block, block), block)
        return pltpu.make_async_copy(src.at[:, at], dst.at[:, at], sems.at[j])

    def mix(j, carry):
        at = pl.ds(pl.multiple_of(j * LANES, LANES), LANES)
        w = [conv_ref[k:k + 1, at] for k in range(taps)]
        for r in range(0, tokens, chunk):
            carried[8 + r:8 + r + chunk] = gates[r:r + chunk] * values[r:r + chunk, at]
        for r in range(0, tokens, chunk):
            now = carried[8 + r:8 + r + chunk]
            conv = w[0] * now
            for k in range(1, taps):
                conv = conv + w[k] * (masks[k - 1, r:r + chunk] * carried[8 + r - k:8 + r - k + chunk])
            sig = 0.5 + 0.5 * jnp.tanh(0.5 * conv)
            silu = conv * sig
            out_ref[r:r + chunk, at] = (hidden_ref[r:r + chunk, at].astype(f32) + now + silu).astype(bf16)
            dconv[r:r + chunk] = cotangent_ref[r:r + chunk, at].astype(f32) * (sig + silu * (1.0 - sig))
        for r in range(0, tokens, chunk):
            dcarried = cotangent_ref[r:r + chunk, at].astype(f32) + w[0] * dconv[r:r + chunk]
            for k in range(1, taps):
                dcarried = dcarried + w[k] * (ahead[k - 1, r:r + chunk] * dconv[r + k:r + k + chunk])
            dvalues[r:r + chunk, at] = (gates[r:r + chunk] * dcarried).astype(bf16)
            dgate[r:r + chunk] += values[r:r + chunk, at] * dcarried
        return carry

    conv_load.wait()

    def mix_block(j, carry):
        load(3, j).wait()
        lax.fori_loop(j * (block // LANES), (j + 1) * (block // LANES), mix, 0)
        write(out_ref, out_hbm, out_sem, j).start()
        return carry

    lax.fori_loop(0, columns // block, mix_block, 0)
    dscore = jnp.sum(dgate[...], axis=1, keepdims=True) * gate * (1.0 - gate) * (1.0 / math.sqrt(columns))
    both = dscore * k_scale * h_scale
    sums[0] = jnp.broadcast_to(both, shape)
    sums[1] = jnp.broadcast_to(both * h_scale * h_scale * cross * inv, shape)
    sums[2] = jnp.broadcast_to(both * k_scale * k_scale * cross * inv, shape)
    total[...] = jnp.zeros_like(total)

    def back(j, carry):
        at = pl.ds(pl.multiple_of(j * block, block), block)
        for c in range(0, block, LANES):
            col = pl.ds(pl.multiple_of(j * block + c, LANES), LANES)
            for r in range(0, tokens, chunk):
                row = slice(r, r + chunk)
                hid = hidden_ref[row, col].astype(f32)
                key = keys[row, col]
                a = sums[0, row]
                grad_ref[row, col] = (
                    cotangent_ref[row, col].astype(f32) + (a * key - sums[1, row] * hid)).astype(bf16)
                dkeys[row, c:c + LANES] = (a * hid - sums[2, row] * key).astype(bf16)
        write(grad_ref, grad_hbm, grad_sem, j).start()
        total[...] += dot(dkeys[...], wk_ref[:, at], NT) + dot(dvalues[:, at], wv_ref[:, at], NT)
        return carry

    lax.fori_loop(0, columns // block, back, 0)
    pieces_ref[...] = total[...].astype(bf16)

    def finish(j, carry):
        write(out_ref, out_hbm, out_sem, j).wait()
        write(grad_ref, grad_hbm, grad_sem, j).wait()
        return carry

    lax.fori_loop(0, columns // block, finish, 0)


def layer(lengths, fetched, hidden, cotangent, w_key, w_value, conv_weight):
    tokens, columns = hidden.shape
    depth = fetched.shape[1]
    taps = conv_weight.shape[0]
    vmem = pl.BlockSpec(memory_space=pltpu.VMEM)
    block = 512 if columns % 512 == 0 else LANES
    return pl.pallas_call(
        layer_kernel,
        out_shape=(
            jax.ShapeDtypeStruct((tokens, columns), bf16),
            jax.ShapeDtypeStruct((tokens, columns), bf16),
            jax.ShapeDtypeStruct((tokens, depth), bf16),
        ),
        in_specs=[pl.BlockSpec(memory_space=pltpu.SMEM), vmem] + [pl.BlockSpec(memory_space=pltpu.HBM)] * 5,
        out_specs=(pl.BlockSpec(memory_space=pl.ANY), pl.BlockSpec(memory_space=pl.ANY), vmem),
        scratch_shapes=[
            pltpu.VMEM((tokens, columns), bf16),
            pltpu.VMEM((tokens, columns), bf16),
            pltpu.VMEM((depth, columns), bf16),
            pltpu.VMEM((depth, columns), bf16),
            pltpu.VMEM((taps, columns), f32),
            pltpu.SemaphoreType.DMA((4, columns // block)),
            pltpu.SemaphoreType.DMA,
            pltpu.VMEM((tokens, columns), bf16),
            pltpu.VMEM((tokens, columns), bf16),
            pltpu.SemaphoreType.DMA((columns // block,)),
            pltpu.SemaphoreType.DMA((columns // block,)),
            pltpu.VMEM((tokens, columns), f32),
            pltpu.VMEM((tokens, columns), f32),
            pltpu.VMEM((tokens, columns), bf16),
            pltpu.VMEM((tokens, block), bf16),
            pltpu.VMEM((taps - 1, tokens, LANES), f32),
            pltpu.VMEM((taps - 1, tokens, LANES), f32),
            pltpu.VMEM((tokens + 8, LANES), f32),
            pltpu.VMEM((tokens + 8, LANES), f32),
            pltpu.VMEM((3, tokens, LANES), f32),
            pltpu.VMEM((tokens, LANES), f32),
            pltpu.VMEM((tokens, LANES), f32),
            pltpu.VMEM((tokens, depth), f32),
        ],
        compiler_params=pltpu.CompilerParams(vmem_limit_bytes=LAYER_VMEM),
        name="layer",
    )(lengths, fetched, hidden, cotangent, w_key, w_value, conv_weight)


def spread_kernel(shards, cap, slots_ref, asked_ref, pieces_ref, grad_ref, outgoing, incoming, send, recv):
    me = lax.axis_index("mem")
    heads, tokens = slots_ref.shape
    rows = grad_ref.shape[0]

    def push(peer):
        return pltpu.make_async_remote_copy(
            src_ref=outgoing.at[peer], dst_ref=incoming.at[me],
            send_sem=send.at[peer], recv_sem=recv.at[me], device_id={"mem": peer})

    def pushed_by(peer):
        return pltpu.make_async_remote_copy(
            src_ref=outgoing.at[peer], dst_ref=incoming.at[peer],
            send_sem=send.at[peer], recv_sem=recv.at[peer], device_id={"mem": peer})

    def pack(peer):
        packed = jnp.zeros((cap, LANES), f32)
        for h in range(heads):
            row = slots_ref[h:h + 1, :] - peer * cap
            hot = one_hot(jnp.broadcast_to(row, (cap, tokens)) == iota((cap, tokens), 0))
            packed = packed + dot(hot, pieces_ref[:, h * LANES:(h + 1) * LANES])
        return packed.astype(bf16)

    greet([{"mem": partner(me, step, shards)} for step in range(1, shards)])

    def send_one(j, carry):
        peer = partner(me, shards - j, shards)
        outgoing[peer] = pack(peer)
        push(peer).start()
        return carry

    lax.fori_loop(1, shards, send_one, 0)
    incoming[me] = pack(me)

    def add(peer):
        half = shards // 2
        row = asked_ref[(peer // half + me // half) % 2, peer % half][:, :cap]
        hot = one_hot(jnp.broadcast_to(row, (rows, cap)) == iota((rows, cap), 0))
        return dot(hot, incoming[peer])

    grad_ref[...] = add(me)

    def take(step, carry):
        peer = partner(me, step, shards)
        pushed_by(peer).wait_recv()
        grad_ref[...] += add(peer)
        return carry

    lax.fori_loop(1, shards, take, 0)

    def finish(step, carry):
        push(partner(me, step, shards)).wait_send()
        return carry

    lax.fori_loop(1, shards, finish, 0)


def spread(slots, asked, pieces, rows, shards, cap):
    vmem = pl.BlockSpec(memory_space=pltpu.VMEM)
    return pl.pallas_call(
        functools.partial(spread_kernel, shards, cap),
        out_shape=jax.ShapeDtypeStruct((rows, LANES), f32),
        in_specs=[vmem] * 3,
        out_specs=vmem,
        scratch_shapes=[
            pltpu.VMEM((shards, cap, LANES), bf16),
            pltpu.VMEM((shards, cap, LANES), bf16),
            pltpu.SemaphoreType.DMA((shards,)),
            pltpu.SemaphoreType.DMA((shards,)),
        ],
        compiler_params=pltpu.CompilerParams(
            collective_id=1, has_side_effects=True, vmem_limit_bytes=SWAP_VMEM),
        name="spread",
    )(slots, asked, pieces)


def local(hidden, cotangent, hash_ids, seq_lengths, hash_table, w_key, w_value, conv_weight):
    shards = lax.axis_size("mem")
    cap = 2 * hash_ids.size // shards
    fetched, slots, asked = fetch(hash_ids.T, hash_table, shards, cap)
    new_hidden, grad_hidden, pieces = layer(
        seq_lengths, fetched, hidden, cotangent, w_key, w_value, conv_weight)
    table_grad = spread(slots, asked, pieces, hash_table.shape[0], shards, cap)
    return new_hidden, grad_hidden, table_grad


def solution(mesh):
    tokens = P(("groups", "mem"), None)
    return jax.shard_map(
        local,
        mesh=mesh,
        in_specs=(tokens, tokens, tokens, tokens, P("mem", None), P(), P(), P()),
        out_specs=(tokens, tokens, tokens),
        check_vma=False,
    )
```

```python
import functools
import math

import jax
import jax.numpy as jnp
from jax import lax
from jax.experimental import pallas as pl
from jax.experimental.pallas import tpu as pltpu
from jax.sharding import PartitionSpec as P

epsilon = 1e-06
LANES = 128
LAYER_VMEM = 60 * 2**20
SWAP_VMEM = 60 * 2**20
SPREAD_VMEM = 52 * 2**20
bf16 = jnp.bfloat16
f32 = jnp.float32
i32 = jnp.int32
NT = (((1,), (1,)), ((), ()))


def dot(a, b, dims=(((1,), (0,)), ((), ()))):
    return lax.dot_general(a, b, dims, preferred_element_type=f32)


def iota(shape, dim):
    return lax.broadcasted_iota(i32, shape, dim)


def one_hot(match):
    return jnp.where(match, 1.0, 0.0).astype(bf16)


def partner(me, step, shards):
    total, bit = 0, 1
    while bit < shards:
        total = total + (((me // bit) % 2 + (step // bit) % 2) % 2) * bit
        bit *= 2
    return total


def greet(peers):
    barrier = pltpu.get_barrier_semaphore()
    for peer in peers:
        pl.semaphore_signal(barrier, inc=1, device_id=peer)
    pl.semaphore_wait(barrier, len(peers))


def as_column(row):
    return jnp.transpose(jnp.broadcast_to(row, (LANES, row.shape[1])))


def fetch_kernel(shards, cap, ids_hbm, table_hbm, fetched_ref, slots_ref, asked_ref,
                 table, mirror, requests, asks, answers, replies, rows32, total, slots_smem, slots_sem,
                 ask_send, ask_recv, row_send, row_recv, far_send, far_recv, swap_send, swap_recv,
                 table_sem, ids_ref, ids_sem):
    me, group = lax.axis_index("mem"), lax.axis_index("groups")
    groups = lax.axis_size("groups")
    half = shards // 2
    home = me // half
    opposite = partner(me, half, shards)
    heads, tokens = ids_ref.shape
    rows = table.shape[0]
    wide = requests.shape[3]
    far = {"mem": opposite}
    twin = {"groups": partner(group, 1, 2) + (group // 2) * 2}
    share = rows // 2 if groups % 2 == 0 else rows
    mine_at = pl.ds(pl.multiple_of((group % 2) * share, 16), share) if share < rows else pl.ds(0, rows)
    twin_at = pl.ds(pl.multiple_of((1 - group % 2) * share, 16), share)

    def remote(src, dst, send, recv, device):
        return pltpu.make_async_remote_copy(
            src_ref=src, dst_ref=dst, send_sem=send, recv_sem=recv, device_id=device)

    def ask(peer, slot):
        at = peer % half
        return remote(requests.at[:, at], asks.at[:, slot], ask_send.at[at], ask_recv.at[slot], {"mem": peer})

    def reply(peer, side, slot):
        at = peer % half
        return remote(answers.at[side, at], replies.at[side, slot],
                      row_send.at[side, at], row_recv.at[side, slot], {"mem": peer})

    here = me % half
    ids_load = pltpu.make_async_copy(ids_hbm, ids_ref, ids_sem)
    ids_load.start()
    greet([{"mem": partner(me, step, shards)} for step in range(1, half)] + [far]
          + ([twin] if share < rows else []))
    to_far = remote(table_hbm.at[mine_at], mirror.at[mine_at], far_send, far_recv, far)
    to_far.start()
    table_load = pltpu.make_async_copy(table_hbm, table, table_sem)
    table_load.start()
    ids_load.wait()

    earlier = one_hot(iota((tokens, tokens), 0) < iota((tokens, tokens), 1))
    seen = jnp.zeros((shards, 1), f32)
    gathered = jnp.zeros((3 * shards, wide), f32)
    for h in range(heads):
        ids = ids_ref[h:h + 1, :]
        owner = ids // rows
        offset = ids - owner * rows
        mine = jnp.where(jnp.broadcast_to(owner, (shards, tokens)) == iota((shards, tokens), 0), 1.0, 0.0)
        ranks = dot(mine.astype(bf16), earlier) + seen
        seen = seen + jnp.sum(mine, axis=1, keepdims=True)
        rank = jnp.sum(mine * ranks, axis=0, keepdims=True).astype(i32)
        slot = owner * cap + rank
        slots_ref[h:h + 1, :] = slot
        at_rank = one_hot(jnp.broadcast_to(rank, (wide, tokens)) == iota((wide, tokens), 0))
        high = (offset // 256).astype(f32)
        low = (offset % 256).astype(f32)
        parts = jnp.concatenate([mine * high, mine * low, mine], axis=0).astype(bf16)
        gathered = gathered + dot(parts, at_rank, NT)
    slots_load = pltpu.make_async_copy(slots_ref, slots_smem, slots_sem)
    slots_load.start()
    wanted = gathered[:shards] * 256.0 + gathered[shards:2 * shards]
    wanted = jnp.where(gathered[2 * shards:] > 0.5, wanted, -1.0).astype(i32)
    for block in range(shards):
        requests[(block // half + home) % 2, block % half] = wanted[block:block + 1, :]

    def ask_all(j, carry):
        ask(partner(me, half - j, shards), here).start()
        return carry

    lax.fori_loop(1, half, ask_all, 0)
    asks[:, here] = requests[:, here]
    table_load.wait()

    def rows_for(side, peer, held):
        column = as_column(asks[side, peer % half])[:cap]
        hot = jnp.concatenate(
            [one_hot(column == iota((cap, LANES), 1) + start) for start in range(0, rows, LANES)], axis=1)
        return dot(hot, held[...]).astype(bf16)

    def answer(j, carry):
        peer = partner(me, half - j, shards)
        ask(peer, peer % half).wait_recv()
        answers[0, peer % half] = rows_for(0, peer, table)
        reply(peer, 0, here).start()
        return carry

    lax.fori_loop(1, half, answer, 0)
    asked_ref[...] = asks[...]

    to_far.wait_recv()
    if share < rows:
        swap = remote(mirror.at[mine_at], mirror.at[mine_at], swap_send, swap_recv, twin)
        swap.start()
    replies[0, here] = rows_for(0, me, table)

    def unpack(side, peer):
        base = ((home + side) % 2 * half + peer % half) * cap
        rows32[pl.ds(pl.multiple_of(base, 16), cap)] = replies[side, peer % half].astype(f32)

    unpack(0, me)
    if share < rows:
        remote(mirror.at[twin_at], mirror.at[twin_at], swap_send, swap_recv, twin).wait_recv()

    def answer_far(j, carry):
        peer = partner(me, half - j, shards)
        answers[1, peer % half] = rows_for(1, peer, mirror)
        reply(peer, 1, here).start()
        return carry

    lax.fori_loop(1, half, answer_far, 0)
    replies[1, here] = rows_for(1, me, mirror)
    unpack(1, me)

    for side in range(2):
        def take(step, carry):
            peer = partner(me, step, shards)
            reply(peer, side, peer % half).wait_recv()
            unpack(side, peer)
            return carry

        lax.fori_loop(1, half, take, 0)
    slots_load.wait()
    group_of = 8

    def pick(j, carry):
        for i in range(group_of):
            token = j * group_of + i
            for h in range(heads):
                total[h, pl.ds(token, 1), :] = rows32[pl.ds(jnp.clip(slots_smem[h, token], 0, shards * cap - 1), 1), :]
        return carry

    lax.fori_loop(0, tokens // group_of, pick, 0)
    for h in range(heads):
        fetched_ref[:, h * LANES:(h + 1) * LANES] = total[h].astype(bf16)

    def finish(step, carry):
        peer = partner(me, step, shards)
        ask(peer, here).wait_send()
        reply(peer, 0, here).wait_send()
        reply(peer, 1, here).wait_send()
        return carry

    lax.fori_loop(1, half, finish, 0)
    to_far.wait_send()
    if share < rows:
        swap.wait_send()


def fetch(ids, table, shards, cap):
    heads, tokens = ids.shape
    rows, width = table.shape
    wide = max(cap, LANES)
    half = shards // 2
    vmem = pl.BlockSpec(memory_space=pltpu.VMEM)
    anywhere = pl.BlockSpec(memory_space=pltpu.HBM)
    dma = pltpu.SemaphoreType.DMA
    return pl.pallas_call(
        functools.partial(fetch_kernel, shards, cap),
        out_shape=(
            jax.ShapeDtypeStruct((tokens, heads * width), bf16),
            jax.ShapeDtypeStruct((heads, tokens), i32),
            jax.ShapeDtypeStruct((2, half, 1, wide), i32),
        ),
        in_specs=[anywhere] * 2,
        out_specs=(vmem, vmem, vmem),
        scratch_shapes=[
            pltpu.VMEM((rows, width), bf16),
            pltpu.VMEM((rows, width), bf16),
            pltpu.VMEM((2, half, 1, wide), i32),
            pltpu.VMEM((2, half, 1, wide), i32),
            pltpu.VMEM((2, half, cap, width), bf16),
            pltpu.VMEM((2, half, cap, width), bf16),
            pltpu.VMEM((shards * cap, width), f32),
            pltpu.VMEM((heads, tokens, width), f32),
            pltpu.SMEM((heads, tokens), i32), dma,
            dma((half,)), dma((half,)), dma((2, half)), dma((2, half)),
            dma, dma, dma, dma, dma, pltpu.VMEM((heads, tokens), i32), dma,
        ],
        compiler_params=pltpu.CompilerParams(
            collective_id=0, has_side_effects=True, vmem_limit_bytes=SWAP_VMEM),
        name="fetch",
    )(ids, table)


def layer_kernel(lengths_ref, fetched_ref, hidden_hbm, cotangent_hbm, wk_hbm, wv_hbm, conv_hbm,
                 out_hbm, grad_hbm, pieces_ref,
                 hidden_ref, cotangent_ref, wk_ref, wv_ref, conv_ref, load_sem, conv_sem,
                 out_ref, grad_ref, out_sem, grad_sem, keys, values, dvalues, dkeys, masks, ahead, carried, dconv,
                 sums, gates, dgate, total):
    tokens, columns = hidden_ref.shape
    taps = conv_ref.shape[0]
    shape = (tokens, LANES)
    block = 512 if columns % 512 == 0 else LANES
    chunk = 128

    def load(which, j):
        src, dst = ((wk_hbm, wk_ref), (wv_hbm, wv_ref), (hidden_hbm, hidden_ref),
                    (cotangent_hbm, cotangent_ref))[which]
        at = pl.ds(pl.multiple_of(j * block, block), block)
        return pltpu.make_async_copy(src.at[:, at], dst.at[:, at], load_sem.at[which, j])

    for j in range(columns // block):
        for which in range(3):
            load(which, j).start()
    conv_load = pltpu.make_async_copy(conv_hbm, conv_ref, conv_sem)
    conv_load.start()
    for j in range(columns // block):
        load(3, j).start()

    def within(position):
        start = jnp.zeros(shape, i32)
        end = 0
        for s in range(lengths_ref.shape[1]):
            length = lengths_ref[0, s]
            end = end + length
            start = start + jnp.where(position >= end, length, 0)
        return position - start

    here = iota(shape, 0)
    for k in range(1, taps):
        masks[k - 1] = jnp.where(within(here) >= k, 1.0, 0.0)
        ahead[k - 1] = jnp.where((within(here + k) >= k) & (here + k < tokens), 1.0, 0.0)
    sums[...] = jnp.zeros_like(sums)
    dgate[...] = jnp.zeros_like(dgate)
    carried[0:8] = jnp.zeros((8, LANES), f32)
    dconv[tokens:tokens + 8] = jnp.zeros((8, LANES), f32)

    def project(j, carry):
        at = pl.ds(pl.multiple_of(j * block, block), block)
        for which in range(3):
            load(which, j).wait()
        key = dot(fetched_ref[...], wk_ref[:, at])
        keys[:, at] = key
        values[:, at] = dot(fetched_ref[...], wv_ref[:, at])
        for c in range(0, block, LANES):
            hid = hidden_ref[:, pl.ds(pl.multiple_of(j * block + c, LANES), LANES)].astype(f32)
            part = key[:, c:c + LANES]
            sums[0] += part * part
            sums[1] += part * hid
            sums[2] += hid * hid
        return carry

    lax.fori_loop(0, columns // block, project, 0)
    inv = 1.0 / columns
    k_scale = lax.rsqrt(jnp.sum(sums[0], axis=1, keepdims=True) * inv + epsilon)
    h_scale = lax.rsqrt(jnp.sum(sums[2], axis=1, keepdims=True) * inv + epsilon)
    cross = jnp.sum(sums[1], axis=1, keepdims=True)
    score = cross * k_scale * h_scale * (1.0 / math.sqrt(columns))
    gate = 0.5 + 0.5 * jnp.tanh(0.5 * score)
    gates[...] = jnp.broadcast_to(gate, shape)

    def write(src, dst, sems, j):
        at = pl.ds(pl.multiple_of(j * block, block), block)
        return pltpu.make_async_copy(src.at[:, at], dst.at[:, at], sems.at[j])

    def mix(j, carry):
        at = pl.ds(pl.multiple_of(j * LANES, LANES), LANES)
        w = [conv_ref[k:k + 1, at] for k in range(taps)]
        for r in range(0, tokens, chunk):
            carried[8 + r:8 + r + chunk] = gates[r:r + chunk] * values[r:r + chunk, at]
        for r in range(0, tokens, chunk):
            now = carried[8 + r:8 + r + chunk]
            conv = w[0] * now
            for k in range(1, taps):
                conv = conv + w[k] * (masks[k - 1, r:r + chunk] * carried[8 + r - k:8 + r - k + chunk])
            sig = 0.5 + 0.5 * jnp.tanh(0.5 * conv)
            silu = conv * sig
            out_ref[r:r + chunk, at] = (hidden_ref[r:r + chunk, at].astype(f32) + now + silu).astype(bf16)
            dconv[r:r + chunk] = cotangent_ref[r:r + chunk, at].astype(f32) * (sig + silu * (1.0 - sig))
        for r in range(0, tokens, chunk):
            dcarried = cotangent_ref[r:r + chunk, at].astype(f32) + w[0] * dconv[r:r + chunk]
            for k in range(1, taps):
                dcarried = dcarried + w[k] * (ahead[k - 1, r:r + chunk] * dconv[r + k:r + k + chunk])
            dvalues[r:r + chunk, at] = (gates[r:r + chunk] * dcarried).astype(bf16)
            dgate[r:r + chunk] += values[r:r + chunk, at] * dcarried
        return carry

    conv_load.wait()

    def mix_block(j, carry):
        load(3, j).wait()
        lax.fori_loop(j * (block // LANES), (j + 1) * (block // LANES), mix, 0)
        write(out_ref, out_hbm, out_sem, j).start()
        return carry

    lax.fori_loop(0, columns // block, mix_block, 0)
    dscore = jnp.sum(dgate[...], axis=1, keepdims=True) * gate * (1.0 - gate) * (1.0 / math.sqrt(columns))
    both = dscore * k_scale * h_scale
    sums[0] = jnp.broadcast_to(both, shape)
    sums[1] = jnp.broadcast_to(both * h_scale * h_scale * cross * inv, shape)
    sums[2] = jnp.broadcast_to(both * k_scale * k_scale * cross * inv, shape)
    total[...] = jnp.zeros_like(total)

    def back(j, carry):
        at = pl.ds(pl.multiple_of(j * block, block), block)
        for c in range(0, block, LANES):
            col = pl.ds(pl.multiple_of(j * block + c, LANES), LANES)
            for r in range(0, tokens, chunk):
                row = slice(r, r + chunk)
                hid = hidden_ref[row, col].astype(f32)
                key = keys[row, col]
                a = sums[0, row]
                grad_ref[row, col] = (
                    cotangent_ref[row, col].astype(f32) + (a * key - sums[1, row] * hid)).astype(bf16)
                dkeys[row, c:c + LANES] = (a * hid - sums[2, row] * key).astype(bf16)
        write(grad_ref, grad_hbm, grad_sem, j).start()
        total[...] += dot(dkeys[...], wk_ref[:, at], NT) + dot(dvalues[:, at], wv_ref[:, at], NT)
        return carry

    lax.fori_loop(0, columns // block, back, 0)
    pieces_ref[...] = total[...].astype(bf16)

    def finish(j, carry):
        write(out_ref, out_hbm, out_sem, j).wait()
        write(grad_ref, grad_hbm, grad_sem, j).wait()
        return carry

    lax.fori_loop(0, columns // block, finish, 0)


def layer(lengths, fetched, hidden, cotangent, w_key, w_value, conv_weight):
    tokens, columns = hidden.shape
    depth = fetched.shape[1]
    taps = conv_weight.shape[0]
    vmem = pl.BlockSpec(memory_space=pltpu.VMEM)
    block = 512 if columns % 512 == 0 else LANES
    return pl.pallas_call(
        layer_kernel,
        out_shape=(
            jax.ShapeDtypeStruct((tokens, columns), bf16),
            jax.ShapeDtypeStruct((tokens, columns), bf16),
            jax.ShapeDtypeStruct((tokens, depth), bf16),
        ),
        in_specs=[pl.BlockSpec(memory_space=pltpu.SMEM), vmem] + [pl.BlockSpec(memory_space=pltpu.HBM)] * 5,
        out_specs=(pl.BlockSpec(memory_space=pl.ANY), pl.BlockSpec(memory_space=pl.ANY), vmem),
        scratch_shapes=[
            pltpu.VMEM((tokens, columns), bf16),
            pltpu.VMEM((tokens, columns), bf16),
            pltpu.VMEM((depth, columns), bf16),
            pltpu.VMEM((depth, columns), bf16),
            pltpu.VMEM((taps, columns), f32),
            pltpu.SemaphoreType.DMA((4, columns // block)),
            pltpu.SemaphoreType.DMA,
            pltpu.VMEM((tokens, columns), bf16),
            pltpu.VMEM((tokens, columns), bf16),
            pltpu.SemaphoreType.DMA((columns // block,)),
            pltpu.SemaphoreType.DMA((columns // block,)),
            pltpu.VMEM((tokens, columns), f32),
            pltpu.VMEM((tokens, columns), f32),
            pltpu.VMEM((tokens, columns), bf16),
            pltpu.VMEM((tokens, block), bf16),
            pltpu.VMEM((taps - 1, tokens, LANES), f32),
            pltpu.VMEM((taps - 1, tokens, LANES), f32),
            pltpu.VMEM((tokens + 8, LANES), f32),
            pltpu.VMEM((tokens + 8, LANES), f32),
            pltpu.VMEM((3, tokens, LANES), f32),
            pltpu.VMEM((tokens, LANES), f32),
            pltpu.VMEM((tokens, LANES), f32),
            pltpu.VMEM((tokens, depth), f32),
        ],
        compiler_params=pltpu.CompilerParams(vmem_limit_bytes=LAYER_VMEM),
        name="layer",
    )(lengths, fetched, hidden, cotangent, w_key, w_value, conv_weight)


def spread_kernel(shards, cap, slots_ref, asked_ref, pieces_ref, grad_ref,
                  outgoing, incoming, partial, landed, send, recv, far_send, far_recv):
    me = lax.axis_index("mem")
    half = shards // 2
    home, here = me // half, me % half
    far = {"mem": partner(me, half, shards)}
    heads, tokens = slots_ref.shape
    rows = grad_ref.shape[0]

    def push(side, peer, slot):
        at = peer % half
        return pltpu.make_async_remote_copy(
            src_ref=outgoing.at[side, at], dst_ref=incoming.at[side, slot],
            send_sem=send.at[side, at], recv_sem=recv.at[side, slot], device_id={"mem": peer})

    def pack(side, peer):
        base = ((home + side) % 2 * half + peer % half) * cap
        packed = jnp.zeros((cap, LANES), f32)
        for h in range(heads):
            row = slots_ref[h:h + 1, :] - base
            hot = one_hot(jnp.broadcast_to(row, (cap, tokens)) == iota((cap, tokens), 0))
            packed = packed + dot(hot, pieces_ref[:, h * LANES:(h + 1) * LANES])
        return packed.astype(bf16)

    def add(side, peer):
        row = asked_ref[side, peer % half][:, :cap]
        hot = one_hot(jnp.broadcast_to(row, (rows, cap)) == iota((rows, cap), 0))
        return dot(hot, incoming[side, peer % half])

    greet([{"mem": partner(me, step, shards)} for step in range(1, half)] + [far])
    to_far = pltpu.make_async_remote_copy(
        src_ref=partial, dst_ref=landed, send_sem=far_send, recv_sem=far_recv, device_id=far)

    for side in (1, 0):
        def send_one(j, carry):
            peer = partner(me, half - j, shards)
            outgoing[side, peer % half] = pack(side, peer)
            push(side, peer, here).start()
            return carry

        lax.fori_loop(1, half, send_one, 0)
        incoming[side, here] = pack(side, me)
        grad_ref[...] = add(side, me)

        def take(step, carry):
            peer = partner(me, step, shards)
            push(side, peer, peer % half).wait_recv()
            grad_ref[...] += add(side, peer)
            return carry

        lax.fori_loop(1, half, take, 0)
        if side == 1:
            partial[...] = grad_ref[...].astype(bf16)
            to_far.start()

    to_far.wait_recv()
    grad_ref[...] += landed[...].astype(f32)

    def finish(step, carry):
        peer = partner(me, step, shards)
        push(0, peer, here).wait_send()
        push(1, peer, here).wait_send()
        return carry

    lax.fori_loop(1, half, finish, 0)
    to_far.wait_send()


def spread(slots, asked, pieces, rows, shards, cap):
    vmem = pl.BlockSpec(memory_space=pltpu.VMEM)
    return pl.pallas_call(
        functools.partial(spread_kernel, shards, cap),
        out_shape=jax.ShapeDtypeStruct((rows, LANES), f32),
        in_specs=[vmem] * 3,
        out_specs=vmem,
        scratch_shapes=[
            pltpu.VMEM((2, shards // 2, cap, LANES), bf16),
            pltpu.VMEM((2, shards // 2, cap, LANES), bf16),
            pltpu.VMEM((rows, LANES), bf16),
            pltpu.VMEM((rows, LANES), bf16),
            pltpu.SemaphoreType.DMA((2, shards // 2)),
            pltpu.SemaphoreType.DMA((2, shards // 2)),
            pltpu.SemaphoreType.DMA,
            pltpu.SemaphoreType.DMA,
        ],
        compiler_params=pltpu.CompilerParams(
            collective_id=1, has_side_effects=True, vmem_limit_bytes=SPREAD_VMEM),
        name="spread",
    )(slots, asked, pieces)


def local(hidden, cotangent, hash_ids, seq_lengths, hash_table, w_key, w_value, conv_weight):
    shards = lax.axis_size("mem")
    cap = 2 * hash_ids.size // shards
    fetched, slots, asked = fetch(hash_ids.T, hash_table, shards, cap)
    new_hidden, grad_hidden, pieces = layer(
        seq_lengths, fetched, hidden, cotangent, w_key, w_value, conv_weight)
    table_grad = spread(slots, asked, pieces, hash_table.shape[0], shards, cap)
    return new_hidden, grad_hidden, table_grad


def solution(mesh):
    tokens = P(("groups", "mem"), None)
    return jax.shard_map(
        local,
        mesh=mesh,
        in_specs=(tokens, tokens, tokens, tokens, P("mem", None), P(), P(), P()),
        out_specs=(tokens, tokens, tokens),
        check_vma=False,
    )
```
